512 devices in a mesh: row: 64 (over x, y, core), col: 8 (over z).
Axes of the slice: x: 4, y: 8, z: 8, core: 2. Of those that a mesh axis runs over, the one named last changes fastest.
Arguments:
- diag_block: float32 [512, 512], P('row'), as said below
- panel: float32 [256, 256, 512], P('row', 'col'), may hold values from -1.5 to 1.5
- panel_mask: int32 [256, 2], P('row'), may hold values 0 or 1
- slot_rows: int32 [64, 4, 16], replicated, may hold values from -1 to 255, as said below
- trail: float32 [256, 16, 256, 256], P('row', None, 'col'), may hold values from -6 to 6
Outputs:
- diag_factor: float32 [512, 512], P('row')
- panel_factor: float32 [256, 256, 512], P('row', 'col')
- trail_out: float32 [256, 16, 256, 256], P('row', None, 'col')
The draws below stay inside these ranges and needn't reach their ends.
Inputs may be any that keep to these rules, and one draw needn't show every extreme that they name: For each r and t, the entries slot_rows[r, t, :] that are not -1 come first and are distinct. For each r, all entries that lie in the tile rows r2 * 4 to r2 * 4 + 3 of one index r2 of row name the same tile row. In every draw some r has no entry -1. `diag_block`: Symmetric; every diagonal entry exceeds the sum of magnitudes of the other entries of its row.
All inputs are finite; a program needn't handle non-finite values. No bound on the sum of `panel_mask` on one device may be relied on, other than what follows from the above.
Results may differ from the reference program's by a relative error of at most 0.0003.
Values sent between devices are 32-bit elements; how exact they have to be, the bound alone decides.
A program may use at most 64 MiB of HBM per device.

```python
import jax
import jax.numpy as jnp
from jax import lax

TILE = 256
TROWS = 4
SLOTS = 16
NTILES = 256
N_ROW = 64


def wendland(scaled_gap):
    inside = jnp.clip(1.0 - scaled_gap, 0.0, 1.0)
    return inside ** 4 * (4.0 * scaled_gap + 1.0)


def draw_diag_block(key, part):
    key = jax.random.fold_in(key, 11)
    subkeys = jax.random.split(key, 3)
    dimension = 2 * TILE
    radius = TILE / 8.0
    bound_sum = 0.0
    for offset_index in range(1, int(radius) + 3):
        scaled_gap = max(offset_index - 0.8, 0.0) / radius
        if scaled_gap < 1.0:
            bound_sum = bound_sum + 2.0 * (1.0 - scaled_gap) ** 4 * (4.0 * scaled_gap + 1.0)
    strength = 0.35
    nugget = 1.02
    dense_total = 0.45
    scales = jnp.exp(jax.random.uniform(subkeys[1], (dimension,), jnp.float32, 0.0, 0.0953))
    amplitude = strength / bound_sum
    level = dense_total / ((dimension - 1) * 1.75)
    indices = jnp.arange(dimension)
    tile_side = indices // TILE
    within = indices % TILE
    jitter = jax.random.uniform(subkeys[0], (dimension,), jnp.float32, -0.4, 0.4)
    location = (2 * within + tile_side).astype(jnp.float32) + jitter
    distance = jnp.abs(location[:, None] - location[None, :]) / radius
    kernel = wendland(distance) * amplitude
    rough_raw = jax.random.uniform(subkeys[2], (dimension, dimension), jnp.float32, -0.75, 0.75)
    rough = 0.5 * (rough_raw + rough_raw.T)
    spread_part = level * (1.0 + rough)
    shaped = jnp.where(indices[:, None] == indices[None, :], nugget, kernel + spread_part)
    matrix = scales[:, None] * scales[None, :] * shaped
    return matrix.astype(jnp.float32)


def draw_slot_rows(key, part):
    subkeys = jax.random.split(key, 4)
    tile_picks = jax.random.randint(subkeys[0], (N_ROW, N_ROW), 0, TROWS)
    scores = jax.random.randint(subkeys[1], (N_ROW, TROWS, N_ROW), 0, 1 << 20) * N_ROW + jnp.arange(N_ROW)
    full_device = jax.random.randint(subkeys[2], (), 0, N_ROW)
    is_full = jnp.arange(N_ROW) == full_device
    last_source = jnp.arange(N_ROW) == N_ROW - 1
    scores = jnp.where(is_full[:, None, None] & last_source[None, None, :], -1, scores)
    tile_picks = jnp.where(is_full[:, None] & last_source[None, :], TROWS - 1, tile_picks)
    ranked = jnp.argsort(scores, axis=-1, stable=True)[:, :, :SLOTS]
    spread_picks = jnp.broadcast_to(tile_picks[:, None, :], (N_ROW, TROWS, N_ROW))
    chosen_tile = jnp.take_along_axis(spread_picks, ranked, axis=-1)
    tile_index = ranked * TROWS + chosen_tile
    least = max(SLOTS // 4, 1)
    counts = jax.random.randint(subkeys[3], (N_ROW, TROWS), least, SLOTS + 1)
    counts = jnp.where(is_full[:, None], SLOTS, counts)
    sparse_device = (full_device + 1) % N_ROW
    sparse_mask = (jnp.arange(N_ROW) == sparse_device)[:, None] & (jnp.arange(TROWS) == 0)[None, :]
    counts = jnp.where(sparse_mask, least, counts)
    return jnp.where(jnp.arange(SLOTS) < counts[:, :, None], tile_index, -1).astype(jnp.int32)


def place_ends(result, stream_key, smallest, high):
    index_at = [jax.random.randint(jax.random.fold_in(stream_key, axis), (), 0, length) for axis, length in enumerate(result.shape)]
    longest = result.shape.index(max(result.shape))
    beside = index_at[:longest] + [(index_at[longest] + 1) % result.shape[longest]] + index_at[longest + 1:]
    return result.at[tuple(index_at)].set(smallest).at[tuple(beside)].set(high)


def block_scale(rng, extent, shards, smallest, high):
    def one(axis_at, blocks):
        draws = jax.random.uniform(jax.random.fold_in(jax.random.fold_in(rng, 6), axis_at), (blocks,), jnp.float32, smallest / len(shards), high / len(shards))
        return jnp.repeat(jnp.exp(draws), extent[axis_at] // blocks).reshape((-1,) + (1,) * (len(extent) - axis_at - 1))

    loudness = one(*shards[0])
    for cut in shards[1:]:
        loudness = loudness * one(*cut)
    return loudness


def normal_values(rng, dims, spread, limit, cuts=(), kind=jnp.bfloat16):
    level = block_scale(rng, dims, cuts, -0.22, 0.18) if cuts else 1.0
    entries = jax.random.normal(rng, dims, jnp.float32) * spread * level
    return jnp.minimum(jnp.maximum(entries, -limit), limit).astype(kind)


def setup_inputs(seed: int = 0) -> dict:
    arg_keys = jax.random.split(jax.random.key(seed), 6)
    return {
        "diag_block": draw_diag_block(jax.random.fold_in(arg_keys[5], 71), 0),
        "panel": normal_values(arg_keys[1], (NTILES, TILE, 2 * TILE), 0.25, 1.5, ((0, 64), (1, 8)), jnp.float32),
        "panel_mask": place_ends((jax.random.randint(arg_keys[2], (NTILES, 2), 0, 2) < 1).astype(jnp.int32), jax.random.fold_in(arg_keys[2], 1), 0, 1),
        "slot_rows": draw_slot_rows(jax.random.fold_in(arg_keys[5], 71), 0),
        "trail": normal_values(arg_keys[4], (NTILES, SLOTS, TILE, TILE), 1.0, 6.0, ((0, 64), (2, 8)), jnp.float32),
    }


def solve_rows(factor_mat, values):
    return jax.scipy.linalg.solve_triangular(factor_mat, values.T, lower=True).T

def reference(diag_block, panel, panel_mask, slot_rows, trail):
    tile_width = trail.shape[-1]
    tile_count = panel.shape[0]
    factor = jnp.linalg.cholesky(diag_block)
    keep_cols = jnp.repeat(panel_mask.astype(jnp.float32), tile_width, axis=1)
    masked = panel * keep_cols[:, None, :]
    solved = solve_rows(factor, masked.reshape(tile_count * tile_width, 2 * tile_width))
    solved = solved.reshape(tile_count, tile_width, 2 * tile_width)
    slot_flat = slot_rows.reshape(tile_count, slot_rows.shape[-1])

    def update(column):
        targets = slot_flat[column]
        live_mask = (targets >= 0).astype(jnp.float32)
        source = jnp.maximum(targets, 0).astype(jnp.int32)
        pieces = solved[source] * live_mask[:, None, None]
        own_tile = solved[column]
        update_term = jnp.einsum('sik,jk->sij', pieces, own_tile, precision=lax.Precision.HIGHEST)
        return trail[column] - update_term
    trail_out = lax.map(update, jnp.arange(tile_count, dtype=jnp.int32))
    return (factor, solved, trail_out)
```

```python
import jax
import jax.numpy as jnp
from jax import lax
from jax.experimental import pallas as pl
from jax.experimental.pallas import tpu as pltpu
from jax.sharding import PartitionSpec as P

MESH = pl.DeviceIdType.MESH
HI = lax.Precision.HIGHEST
NX, NY, NK, NZ = 4, 8, 2, 8
TILES, SLAB, WIDTH, TW = 4, 32, 512, 256
RB, RA = 24, 8
SLOTS = 16


def dot32(a, b, tb=False):
    dims = (((1,), (1 if tb else 0,)), ((), ()))
    return lax.dot_general(a, b, dims, precision=HI, preferred_element_type=jnp.float32)


def dot16(a, b):
    dims = (((1,), (1,)), ((), ()))
    return lax.dot_general(a, b, dims, preferred_element_type=jnp.float32)


def split(x):
    hi = x.astype(jnp.bfloat16)
    lo = (x - hi.astype(jnp.float32)).astype(jnp.bfloat16)
    return hi, lo


def lanes(x, lane):
    return jnp.broadcast_to(x[:, lane : lane + 1], x.shape)


def rows(x, row):
    return jnp.broadcast_to(x[row : row + 1, :], (8, 128))


def total(xs):
    while len(xs) > 1:
        xs = [xs[i] + xs[i + 1] if i + 1 < len(xs) else xs[i] for i in range(0, len(xs), 2)]
    return xs[0]


def pivot8(cols):
    d, low, rs, inv = {}, {}, {}, {}
    for b in range(8):
        for a in range(b, 8):
            d[a, b] = rows(cols[b], a)
    for k in range(8):
        rs[k] = lax.rsqrt(d[k, k])
        for i in range(k + 1, 8):
            low[i, k] = d[i, k] * rs[k]
        for i in range(k + 1, 8):
            for j in range(k + 1, i + 1):
                d[i, j] = d[i, j] - low[i, k] * low[j, k]
        inv[k, k] = rs[k]
        for m in range(k):
            s = low[k, m] * inv[m, m]
            for q in range(m + 1, k):
                s = s + low[k, q] * inv[q, m]
            inv[k, m] = -(rs[k] * s)
    return inv


def sweep8(j, m_ref, lt_ref):
    r0 = j * 8
    sub = lax.broadcasted_iota(jnp.int32, (8, 128), 0)
    lane = lax.broadcasted_iota(jnp.int32, (8, 128), 1)
    block = m_ref[r0 : r0 + 8, :]
    inv = pivot8([lanes(block, r0 + b) for b in range(8)])
    zero = jnp.zeros((8, 128), jnp.float32)
    colv, rowv = [], []
    for m in range(8):
        v = zero
        for k in range(m, 8):
            v = jnp.where(sub == k, inv[k, m], v)
        colv.append(v)
    for k in range(8):
        v = zero
        for m in range(k + 1):
            v = jnp.where(sub == m, inv[k, m], v)
        rowv.append(v)
    inside = (lane >= r0) & (lane < r0 + 8)
    u = total([colv[m] * rows(block, m) for m in range(8)])
    lt_ref[r0 : r0 + 8, :] = jnp.where(lane >= r0 + sub, u, 0.0)
    pattern = zero
    for m in range(8):
        pattern = jnp.where(lane == r0 + m, colv[m], pattern)
    u = jnp.where(inside, pattern, u)
    p = total([rowv[k] * rows(u, k) for k in range(8)])
    spread = [rows(p, m) for m in range(8)]
    m_ref[r0 : r0 + 8, :] = u
    for i in range(j + 1, 16):
        mi = m_ref[8 * i : 8 * i + 8, :]
        upd = total([lanes(mi, r0 + m) * spread[m] for m in range(8)])
        m_ref[8 * i : 8 * i + 8, :] = jnp.where(inside, 0.0, mi) - upd


def block_update(J, a_ref, lt_ref, blk, ltb):
    r0, r1 = J * 128, J * 128 + 128
    tri = lax.broadcasted_iota(jnp.int32, (128, 128), 0) >= lax.broadcasted_iota(jnp.int32, (128, 128), 1)
    linv = jnp.where(tri, blk[...], 0.0)
    lt_ref[r0:r1, r0:r1] = ltb[...]
    if J > 0:
        lt_ref[r0:r1, :r0] = jnp.zeros((128, r0), jnp.float32)
        uw = dot32(linv, a_ref[r0:r1, :r0])
        a_ref[r0:r1, :r0] = uw
    if J < 3:
        lcol = dot32(a_ref[r1:, r0:r1], linv, tb=True)
        ut = dot32(linv, a_ref[r0:r1, r1:])
        lt_ref[r0:r1, r1:] = ut
        a_ref[r1:, r1:] = a_ref[r1:, r1:] - dot32(lcol, ut)
        a_ref[r1:, r0:r1] = -dot32(lcol, linv)
        if J > 0:
            a_ref[r1:, :r0] = a_ref[r1:, :r0] - dot32(lcol, uw)
        a_ref[r0:r1, r1:] = jnp.zeros((128, 512 - r1), jnp.float32)
    a_ref[r0:r1, r0:r1] = linv


def kernel(
    diag_ref, panel_ref, mask_ref, table_ref, slot_ref, trail_ref,
    factor_ref, solved_ref, out_ref,
    a5, w, lt, blk, ltb, xa, zg, yb0, yb1, yb2, yb3, yb4, yb5, yb6, yb7,
    sb, sa, pb, pa, bhi, blo, lhi, llo, trail_v, out_v,
    dy_s, dy_r, dx_s, dx_r, dk_s, dk_r, xa_s, xa_r, z_s, z_r, y_s, y_r, sb_s, sb_r, sa_s, sa_r, t_sem, o_sem,
):
    me = lax.axis_index("row")
    z = lax.axis_index("col")
    x, y, k = me // 16, (me // 2) % 8, me % 2

    def dev(dx=0, dy=0, dk=0, dz=0):
        return (((x + dx) % 4 * 8 + (y + dy) % 8) * 2 + (k + dk) % 2, (z + dz) % 8)

    def remote(src, dst, ss, rs, to):
        return pltpu.make_async_remote_copy(src, dst, ss, rs, device_id=to, device_id_type=MESH)

    trail_in = [
        pltpu.make_async_copy(trail_ref.at[t], trail_v.at[t], t_sem.at[t]) for t in range(TILES)
    ]
    for c in trail_in:
        c.start()

    first_half = lax.broadcasted_iota(jnp.int32, (SLAB, WIDTH), 1) < TW
    for t in range(TILES):
        keep = jnp.where(first_half, mask_ref[t, 0].astype(jnp.float32), mask_ref[t, 1].astype(jnp.float32))
        v = panel_ref[t] * keep
        zg[t, pl.ds(z, 1)] = v[None]
        yb0[t] = v[:RB]
        xa[pl.ds(x, 1), t] = v[RB:][None]
    a5[pl.ds(x, 1), pl.ds(y, 1), pl.ds(k, 1)] = diag_ref[...][None, None, None]

    barrier = pltpu.get_barrier_semaphore()
    partners = [dev(dz=1), dev(dz=-1)]
    partners += [dev(dx=e // 2, dk=e % 2) for e in range(1, 8)]
    partners += [dev(dy=e // 2, dk=e % 2) for e in range(2, 16)]
    for to in partners:
        pl.semaphore_signal(barrier, inc=1, device_id=to, device_id_type=MESH)
    pl.semaphore_wait(barrier, len(partners))

    def dy_copy(i):
        return remote(diag_ref, a5.at[x, y, k], dy_s.at[i], dy_r.at[i], dev(dy=i + 1))

    def dx_copy(c, i):
        ref = a5.at[x, :, k, :, pl.ds(c * 128, 128)]
        return remote(ref, ref, dx_s.at[c, i], dx_r.at[c, i], dev(dx=i + 1))

    def dk_copy(c):
        ref = a5.at[:, :, k, :, pl.ds(c * 128, 128)]
        return remote(ref, ref, dk_s.at[c], dk_r.at[c], dev(dk=1))

    for i in range(7):
        dy_copy(i).start()

    yb = [yb0, yb1, yb2, yb3, yb4, yb5, yb6, yb7]
    step_of = {0: 0, 1: -1, 2: -2, 3: -3, 4: 1, 5: 2, 6: 3, 7: 4}

    def ring(step, way):
        src = 0 if step == 0 else (step if way == 0 else step + 3)
        dst = 7 if step == 3 else (step + 1 if way == 0 else step + 4)
        part = pl.ds(0, TILES) if step < 3 else pl.ds(2 * way, 2)
        return src, dst, part

    def z_copy(step, way):
        src, _, part = ring(step, way)
        block = (z + step_of[src]) % 8
        ref = zg.at[part, block]
        return remote(ref, ref, z_s.at[step, way], z_r.at[step, way], dev(dz=1 if way == 0 else -1))

    def y_copy(step, way):
        src, dst, part = ring(step, way)
        return remote(
            yb[src].at[part], yb[dst].at[part], y_s.at[step, way], y_r.at[step, way],
            dev(dy=1 if way == 0 else -1),
        )

    def xa_copy(i):
        return remote(xa.at[x], xa.at[x], xa_s.at[i], xa_r.at[i], dev(dx=i + 1))

    for way in range(2):
        z_copy(0, way).start()
        y_copy(0, way).start()
    for i in range(3):
        xa_copy(i).start()

    def sb_copy(pos, e, yy):
        return remote(
            sb.at[e, pos], pb.at[x, k, yy], sb_s.at[e, pos], sb_r.at[e, pos],
            dev(dx=(e + 1) // 2, dk=(e + 1) % 2),
        )

    def send_block(pos):
        yy = (y + step_of[pos]) % 8
        source = (x * 8 + yy) * 2 + k
        buf = yb[pos]
        pb[x, k, yy] = buf[table_ref[me, source]]

        def body(e, c):
            to = dev(dx=(e + 1) // 2, dk=(e + 1) % 2)[0]
            sb[e, pos] = buf[table_ref[to, source]]
            sb_copy(pos, e, yy).start()
            return c

        lax.fori_loop(0, 7, body, 0)

    def sa_copy(e):
        return remote(
            sa.at[e], pa.at[y, k], sa_s.at[e], sa_r.at[e], dev(dy=(e + 1) // 2, dk=(e + 1) % 2)
        )

    def send_cross():
        for xx in range(NX):
            pa[y, k, xx] = xa[xx, table_ref[me, (xx * 8 + y) * 2 + k]]

        def body(e, c):
            to = dev(dy=(e + 1) // 2, dk=(e + 1) % 2)[0]
            for xx in range(NX):
                sa[e, xx] = xa[xx, table_ref[to, (xx * 8 + y) * 2 + k]]
            sa_copy(e).start()
            return c

        lax.fori_loop(0, 15, body, 0)

    def service(step):
        for way in range(2):
            y_copy(step, way).wait_recv()
            if step < 3:
                y_copy(step + 1, way).start()
        for way in range(2):
            z_copy(step, way).wait_recv()
            if step < 3:
                z_copy(step + 1, way).start()
        if step < 3:
            send_block(step + 1)
            send_block(step + 4)
        else:
            send_block(7)

    for i in range(7):
        dy_copy(i).wait_recv()
    for c in range(4):
        for i in range(3):
            dx_copy(c, i).start()
    send_block(0)
    for i in range(3):
        xa_copy(i).wait_recv()
    send_cross()
    for c in range(4):
        for i in range(3):
            dx_copy(c, i).wait_recv()
        dk_copy(c).start()
    for c in range(4):
        dk_copy(c).wait_recv()
    for xx in range(NX):
        w[xx * 128 : xx * 128 + 128, :] = a5[xx].reshape(128, 512)
    service(0)

    def factor_block(J, carry):
        r0 = pl.multiple_of(J * 128, 128)
        blk[...] = w[pl.ds(r0, 128), pl.ds(r0, 128)]
        for j in range(16):
            sweep8(j, blk, ltb)
        for s in range(4):

            @pl.when(J == s)
            def _(s=s):
                block_update(s, w, lt, blk, ltb)
                if s < 3:
                    service(s + 1)

        return carry

    lax.fori_loop(0, 4, factor_block, 0)

    pick = lax.broadcasted_iota(jnp.int32, (8, 512), 1) == me * 8 + lax.broadcasted_iota(jnp.int32, (8, 512), 0)
    factor_ref[...] = dot32(pick.astype(jnp.float32), lt[...], tb=True)
    own = zg[:, pl.ds(z, 1)].reshape(TILES * SLAB, WIDTH)
    solved_ref[...] = dot32(own, w[...], tb=True).reshape(TILES, SLAB, WIDTH)
    wv = w[...]
    lt[...] = lax.dot_general(
        wv, wv, (((0,), (0,)), ((), ())), precision=HI, preferred_element_type=jnp.float32
    )
    for t in range(TILES):
        bhi[t], blo[t] = split(dot32(zg[t].reshape(TW, WIDTH), lt[...]))

    for pos in range(8):
        yy = (y + step_of[pos]) % 8
        for e in range(7):
            sb_copy(pos, e, yy).wait_recv()
    for e in range(15):
        sa_copy(e).wait_recv()

    def update(t, carry):
        live = []
        for s in range(SLOTS):
            p = slot_ref[t, s]
            live.append((p >= 0).astype(jnp.float32))
            src = jnp.maximum(p, 0) // TILES
            x2, y2, k2 = src // 16, (src // 2) % 8, src % 2
            v = jnp.concatenate([pb[x2, k2, y2], pa[y2, k2, x2]], axis=0)
            hi, lo = split(v)
            lhi[s * SLAB : s * SLAB + SLAB, :] = hi
            llo[s * SLAB : s * SLAB + SLAB, :] = lo
        bh, bl = bhi[t], blo[t]
        upd = dot16(lhi[...], bh) + (dot16(lhi[...], bl) + dot16(llo[...], bh))
        pltpu.make_async_copy(trail_ref.at[t], trail_v.at[t], t_sem.at[t]).wait()
        for s in range(SLOTS):
            out_v[t, s] = trail_v[t, s] - upd[s * SLAB : s * SLAB + SLAB] * live[s]
        pltpu.make_async_copy(out_v.at[t], out_ref.at[t], o_sem.at[t]).start()
        return carry

    lax.fori_loop(0, TILES, update, 0)

    for i in range(7):
        dy_copy(i).wait_send()
    for c in range(4):
        for i in range(3):
            dx_copy(c, i).wait_send()
        dk_copy(c).wait_send()
    for i in range(3):
        xa_copy(i).wait_send()
    for step in range(4):
        for way in range(2):
            z_copy(step, way).wait_send()
            y_copy(step, way).wait_send()
    for pos in range(8):
        yy = (y + step_of[pos]) % 8
        for e in range(7):
            sb_copy(pos, e, yy).wait_send()
    for e in range(15):
        sa_copy(e).wait_send()
    for t in range(TILES):
        pltpu.make_async_copy(out_v.at[t], out_ref.at[t], o_sem.at[t]).wait()


def per_device(diag_block, panel, panel_mask, slot_rows, trail):
    n_row = slot_rows.shape[0]
    me = lax.axis_index("row")
    slots = slot_rows.reshape(n_row, -1)
    match = (slots >> 2)[:, :, None] == jnp.arange(n_row, dtype=jnp.int32)
    table = jnp.max(jnp.where(match, (slots & 3)[:, :, None], 0), axis=1)
    my_slots = lax.dynamic_index_in_dim(slot_rows, me, 0, keepdims=False)
    f32 = jnp.float32
    vm = lambda *shape: pltpu.VMEM(shape, f32)
    dma = lambda *shape: pltpu.SemaphoreType.DMA(shape)
    bf = lambda *shape: pltpu.VMEM(shape, jnp.bfloat16)
    vmem = pl.BlockSpec(memory_space=pltpu.VMEM)
    smem = pl.BlockSpec(memory_space=pltpu.SMEM)
    hbm = pl.BlockSpec(memory_space=pl.ANY)
    return pl.pallas_call(
        kernel,
        out_shape=(
            jax.ShapeDtypeStruct(diag_block.shape, f32),
            jax.ShapeDtypeStruct(panel.shape, f32),
            jax.ShapeDtypeStruct(trail.shape, f32),
        ),
        in_specs=[vmem, vmem, smem, smem, smem, hbm],
        out_specs=(vmem, vmem, hbm),
        scratch_shapes=[
            vm(NX, NY, NK, 8, WIDTH), vm(512, 512), vm(512, 512), vm(128, 128), vm(128, 128),
            vm(NX, TILES, RA, WIDTH), vm(TILES, NZ, SLAB, WIDTH),
            *[vm(TILES, RB, WIDTH) for _ in range(8)],
            vm(7, 8, RB, WIDTH), vm(15, NX, RA, WIDTH),
            vm(NX, NK, NY, RB, WIDTH), vm(NY, NK, NX, RA, WIDTH),
            bf(TILES, TW, WIDTH), bf(TILES, TW, WIDTH), bf(SLOTS * SLAB, WIDTH), bf(SLOTS * SLAB, WIDTH),
            vm(TILES, SLOTS, SLAB, TW), vm(TILES, SLOTS, SLAB, TW),
            dma(7), dma(7), dma(4, 3), dma(4, 3), dma(4), dma(4), dma(3), dma(3),
            dma(4, 2), dma(4, 2), dma(4, 2), dma(4, 2), dma(7, 8), dma(7, 8), dma(15), dma(15),
            dma(4), dma(4),
        ],
        compiler_params=pltpu.CompilerParams(
            collective_id=0, has_side_effects=True, vmem_limit_bytes=56 * 1024 * 1024
        ),
        name="panels",
    )(diag_block, panel, panel_mask, table, my_slots, trail)


def solution(mesh):
    in_specs = (
        P("row", None),
        P("row", "col", None),
        P("row", None),
        P(),
        P("row", None, "col", None),
    )
    out_specs = (P("row", None), P("row", "col", None), P("row", None, "col", None))
    return jax.shard_map(
        per_device, mesh=mesh, in_specs=in_specs, out_specs=out_specs, check_vma=False
    )
```

```python
import jax
import jax.numpy as jnp
from jax import lax
from jax.experimental import pallas as pl
from jax.experimental.pallas import tpu as pltpu
from jax.sharding import PartitionSpec as P

MESH = pl.DeviceIdType.MESH
HI = lax.Precision.HIGHEST
NX, NY, NK, NZ = 4, 8, 2, 8
TILES, SLAB, WIDTH, TW = 4, 32, 512, 256
RB, RA = 24, 8
SLOTS = 16


def dot32(a, b, tb=False):
    dims = (((1,), (1 if tb else 0,)), ((), ()))
    return lax.dot_general(a, b, dims, precision=HI, preferred_element_type=jnp.float32)


def dot16(a, b):
    dims = (((1,), (1,)), ((), ()))
    return lax.dot_general(a, b, dims, preferred_element_type=jnp.float32)


def split(x):
    hi = x.astype(jnp.bfloat16)
    lo = (x - hi.astype(jnp.float32)).astype(jnp.bfloat16)
    return hi, lo


def dot48(a, b, tb=False):
    dims = (((1,), (1 if tb else 0,)), ((), ()))
    ah, al = split(a)
    bh, bl = split(b)
    dot = lambda p, q: lax.dot_general(p, q, dims, preferred_element_type=jnp.float32)
    return dot(ah, bh) + (dot(ah, bl) + dot(al, bh))


def lanes(x, lane):
    return jnp.broadcast_to(x[:, lane : lane + 1], x.shape)


def rows(x, row):
    return jnp.broadcast_to(x[row : row + 1, :], (8, 128))


def total(xs):
    while len(xs) > 1:
        xs = [xs[i] + xs[i + 1] if i + 1 < len(xs) else xs[i] for i in range(0, len(xs), 2)]
    return xs[0]


def pivot8(cols):
    d, low, rs, inv = {}, {}, {}, {}
    for b in range(8):
        for a in range(b, 8):
            d[a, b] = rows(cols[b], a)
    for k in range(8):
        rs[k] = lax.rsqrt(d[k, k])
        for i in range(k + 1, 8):
            low[i, k] = d[i, k] * rs[k]
        for i in range(k + 1, 8):
            for j in range(k + 1, i + 1):
                d[i, j] = d[i, j] - low[i, k] * low[j, k]
        inv[k, k] = rs[k]
        for m in range(k):
            s = low[k, m] * inv[m, m]
            for q in range(m + 1, k):
                s = s + low[k, q] * inv[q, m]
            inv[k, m] = -(rs[k] * s)
    return inv


def sweep8(j, m_ref, lt_ref):
    r0 = j * 8
    sub = lax.broadcasted_iota(jnp.int32, (8, 128), 0)
    lane = lax.broadcasted_iota(jnp.int32, (8, 128), 1)
    block = m_ref[r0 : r0 + 8, :]
    inv = pivot8([lanes(block, r0 + b) for b in range(8)])
    zero = jnp.zeros((8, 128), jnp.float32)
    colv, rowv = [], []
    for m in range(8):
        v = zero
        for k in range(m, 8):
            v = jnp.where(sub == k, inv[k, m], v)
        colv.append(v)
    for k in range(8):
        v = zero
        for m in range(k + 1):
            v = jnp.where(sub == m, inv[k, m], v)
        rowv.append(v)
    inside = (lane >= r0) & (lane < r0 + 8)
    u = total([colv[m] * rows(block, m) for m in range(8)])
    lt_ref[r0 : r0 + 8, :] = jnp.where(lane >= r0 + sub, u, 0.0)
    pattern = zero
    for m in range(8):
        pattern = jnp.where(lane == r0 + m, colv[m], pattern)
    u = jnp.where(inside, pattern, u)
    p = total([rowv[k] * rows(u, k) for k in range(8)])
    spread = [rows(p, m) for m in range(8)]
    m_ref[r0 : r0 + 8, :] = u
    for i in range(j + 1, 16):
        mi = m_ref[8 * i : 8 * i + 8, :]
        upd = total([lanes(mi, r0 + m) * spread[m] for m in range(8)])
        m_ref[8 * i : 8 * i + 8, :] = jnp.where(inside, 0.0, mi) - upd


def block_update(J, a_ref, lt_ref, blk, ltb):
    r0, r1 = J * 128, J * 128 + 128
    tri = lax.broadcasted_iota(jnp.int32, (128, 128), 0) >= lax.broadcasted_iota(jnp.int32, (128, 128), 1)
    linv = jnp.where(tri, blk[...], 0.0)
    lt_ref[r0:r1, r0:r1] = ltb[...]
    if J > 0:
        uw = dot32(linv, a_ref[r0:r1, :r0])
        a_ref[r0:r1, :r0] = uw
    if J < 3:
        lcol = dot32(a_ref[r1:, r0:r1], linv, tb=True)
        ut = lcol.T
        lt_ref[r0:r1, r1:] = ut
        a_ref[r1:, r1:] = a_ref[r1:, r1:] - dot32(lcol, ut)
        a_ref[r1:, r0:r1] = -dot32(lcol, linv)
        if J > 0:
            a_ref[r1:, :r0] = a_ref[r1:, :r0] - dot32(lcol, uw)
    a_ref[r0:r1, r0:r1] = linv
    if J < 3:
        a_ref[r0:r1, r1:] = jnp.zeros((128, 512 - r1), jnp.float32)


def kernel(
    diag_ref, panel_ref, mask_ref, slots_ref, trail_ref,
    factor_ref, solved_ref, out_ref,
    a7, w, lt, blk, ltb, xa, zg, yb0, yb1, yb2, yb3, yb4, yb5, yb6, yb7,
    sb, sa, pb, pa, bhi, blo, ph, pll, trail_v, out_v, panel_v, mask_v, slots_v, slots_s, table_v, table_s,
    dy_s, dy_r, dx_s, dx_r, dk_s, dk_r, xa_s, xa_r, z_s, z_r, y_s, y_r, sb_s, sb_r, sa_s, sa_r, l_sem, t_sem, o_sem,
):
    me = lax.axis_index("row")
    z = lax.axis_index("col")
    x, y, k = me // 16, (me // 2) % 8, me % 2

    def dev(dx=0, dy=0, dk=0, dz=0):
        return (((x + dx) % 4 * 8 + (y + dy) % 8) * 2 + (k + dk) % 2, (z + dz) % 8)

    def remote(src, dst, ss, rs, to):
        return pltpu.make_async_remote_copy(src, dst, ss, rs, device_id=to, device_id_type=MESH)

    loads = [
        pltpu.make_async_copy(diag_ref.at[:, pl.ds(c * 128, 128)], a7.at[c, k, x, y], l_sem.at[c])
        for c in range(4)
    ]
    loads += [
        pltpu.make_async_copy(panel_ref, panel_v, l_sem.at[4]),
        pltpu.make_async_copy(mask_ref, mask_v, l_sem.at[5]),
        pltpu.make_async_copy(slots_ref, slots_v, l_sem.at[6]),
        pltpu.make_async_copy(slots_ref, slots_s, l_sem.at[8]),
    ]
    for c in loads:
        c.start()
    trail_in = [pltpu.make_async_copy(trail_ref.at[t], trail_v.at[t], t_sem.at[t]) for t in range(TILES)]
    trail_out = [pltpu.make_async_copy(out_v.at[t], out_ref.at[t], o_sem.at[t]) for t in range(TILES)]

    barrier = pltpu.get_barrier_semaphore()
    partners = [dev(dz=1), dev(dz=-1)]
    partners += [dev(dx=e // 2, dk=e % 2) for e in range(1, 8)]
    partners += [dev(dy=e // 2, dk=e % 2) for e in range(2, 16)]
    for to in partners:
        pl.semaphore_signal(barrier, inc=1, device_id=to, device_id_type=MESH)
    for c in loads[:6]:
        c.wait()

    first_half = lax.broadcasted_iota(jnp.int32, (SLAB, WIDTH), 1) < TW
    mask = mask_v[...].astype(jnp.float32)
    for t in range(TILES):
        keep = jnp.where(
            first_half,
            jnp.broadcast_to(mask[0:1, t : t + 1], (SLAB, WIDTH)),
            jnp.broadcast_to(mask[1:2, t : t + 1], (SLAB, WIDTH)),
        )
        v = panel_v[t] * keep
        zg[t, pl.ds(z, 1)] = v[None]
        yb0[t] = v[:RB]
        xa[pl.ds(x, 1), t] = v[RB:][None]
    pl.semaphore_wait(barrier, len(partners))

    def dy_copy(c, i):
        ref = a7.at[c, k, x, y]
        return remote(ref, ref, dy_s.at[c], dy_r.at[c], dev(dy=i + 1))

    def dx_copy(c, i):
        ref = a7.at[c, k, x]
        return remote(ref, ref, dx_s.at[c], dx_r.at[c, i], dev(dx=i + 1))

    def dy_all(c):
        ref = a7.at[c, k, x, pl.ds(0, 7)]
        return remote(ref, ref, dy_s.at[c], dy_r.at[c], dev(dy=1))

    def dx_all(c):
        ref = a7.at[c, k, pl.ds(0, 3)]
        return remote(ref, ref, dx_s.at[c], dx_r.at[c, 0], dev(dx=1))

    def dk_copy(c):
        ref = a7.at[c, k, pl.ds(c, 4 - c)]
        return remote(ref, ref, dk_s.at[c], dk_r.at[c], dev(dk=1))

    def start_dy(c):
        @pl.when(x >= c)
        def _():
            for i in range(7):
                dy_copy(c, i).start()

    start_dy(0)

    yb = [yb0, yb1, yb2, yb3, yb4, yb5, yb6, yb7]
    step_of = {0: 0, 1: -1, 2: -2, 3: -3, 4: 1, 5: 2, 6: 3, 7: 4}

    def ring(step, way):
        src = 0 if step == 0 else (step if way == 0 else step + 3)
        dst = 7 if step == 3 else (step + 1 if way == 0 else step + 4)
        part = pl.ds(0, TILES) if step < 3 else pl.ds(2 * way, 2)
        return src, dst, part

    def z_copy(step, way):
        src, _, part = ring(step, way)
        block = (z + step_of[src]) % 8
        ref = zg.at[part, block]
        return remote(ref, ref, z_s.at[step, way], z_r.at[step, way], dev(dz=1 if way == 0 else -1))

    def y_copy(step, way):
        src, dst, part = ring(step, way)
        return remote(
            yb[src].at[part], yb[dst].at[part], y_s.at[step, way], y_r.at[step, way],
            dev(dy=1 if way == 0 else -1),
        )

    def xa_copy(i):
        return remote(xa.at[x], xa.at[x], xa_s, xa_r, dev(dx=i + 1))

    xa_all = remote(xa.at[pl.ds(0, 3)], xa.at[pl.ds(0, 3)], xa_s, xa_r, dev(dx=1))
    for way in range(2):
        y_copy(0, way).start()
    for c in range(1, 4):
        start_dy(c)
    for i in range(3):
        xa_copy(i).start()
    for way in range(2):
        z_copy(0, way).start()

    loads[6].wait()
    wanted = slots_v[...].reshape(TILES * SLOTS, 64)
    source_row, tile = wanted >> 2, wanted & 3
    sub16 = lax.broadcasted_iota(jnp.int32, (16, 64), 0)
    table = jnp.zeros((16, 64), jnp.int32)
    for i in range(12):
        src = (x * 8 + i) * 2 + k if i < 8 else ((i - 8) * 8 + y) * 2 + k
        best = jnp.max(jnp.where(source_row == src, tile, 0), axis=0, keepdims=True)
        table = jnp.where(sub16 == i, best, table)
    table_v[...] = table
    to_scalar = pltpu.make_async_copy(table_v, table_s, l_sem.at[7])
    to_scalar.start()

    def sb_copy(pos, e, yy):
        return remote(
            sb.at[e, pos], pb.at[x, k, yy], sb_s, sb_r.at[pos],
            dev(dx=(e + 1) // 2, dk=(e + 1) % 2),
        )

    def send_block(pos):
        yy = (y + step_of[pos]) % 8
        buf = yb[pos]
        pb[x, k, yy] = buf[table_s[yy, me]]

        def body(e, c):
            to = dev(dx=(e + 1) // 2, dk=(e + 1) % 2)[0]
            sb[e, pos] = buf[table_s[yy, to]]
            sb_copy(pos, e, yy).start()
            return c

        lax.fori_loop(0, 7, body, 0)

    def sa_copy(e):
        return remote(
            sa.at[e], pa.at[y, k], sa_s, sa_r.at[(e + 1) // 2], dev(dy=(e + 1) // 2, dk=(e + 1) % 2)
        )

    def send_cross(lo, hi):
        def body(e, c):
            to = dev(dy=(e + 1) // 2, dk=(e + 1) % 2)[0]
            for xx in range(NX):
                sa[e, xx] = xa[xx, table_s[8 + xx, to]]
            sa_copy(e).start()
            return c

        lax.fori_loop(lo, hi, body, 0)

    def service(step):
        for way in range(2):
            y_copy(step, way).wait_recv()
            if step < 3:
                y_copy(step + 1, way).start()
        for way in range(2):
            z_copy(step, way).wait_recv()
            if step < 3:
                z_copy(step + 1, way).start()
        if step < 3:
            send_block(step + 1)
            send_block(step + 4)
        else:
            send_block(7)
        send_cross(4 * step, min(4 * step + 4, 15))

    def turn_diag(c):
        @pl.when(x >= c)
        def _():
            dy_all(c).wait_recv()
            for i in range(3):
                dx_copy(c, i).start()

    def pass_diag(c):
        for i in range(3):

            @pl.when((x + 3 - i) % 4 >= c)
            def _(i=i):
                dx_copy(c, i).wait_recv()

        dk_copy(c).start()

    def unpack(c):
        dk_copy(c).wait_recv()
        for xx in range(c, NX):
            v = jnp.stack([a7[c, 0, xx], a7[c, 1, xx]], axis=1)
            w[xx * 128 : xx * 128 + 128, c * 128 : c * 128 + 128] = v.reshape(128, 128)

    w[...] = jnp.zeros_like(w)
    lt[...] = jnp.zeros_like(lt)
    for c in range(4):
        turn_diag(c)
    to_scalar.wait()
    send_block(0)
    xa_all.wait_recv()
    for xx in range(NX):
        pa[y, k, xx] = xa[xx, table_s[8 + xx, me]]
    pass_diag(0)
    service(0)
    unpack(0)

    def factor_block(J, carry):
        r0 = pl.multiple_of(J * 128, 128)
        blk[...] = w[pl.ds(r0, 128), pl.ds(r0, 128)]
        for j in range(16):
            if j == 5:

                @pl.when(J == 0)
                def _():
                    for c in range(1, 4):
                        pass_diag(c)

            if j == 8:

                @pl.when(J == 2)
                def _():
                    service(2)

            sweep8(j, blk, ltb)
        for s in range(4):

            @pl.when(J == s)
            def _(s=s):
                if s == 0:
                    for c in range(1, 4):
                        unpack(c)
                block_update(s, w, lt, blk, ltb)
                if s == 0:
                    service(1)
                if s == 3:
                    service(3)

        return carry

    lax.fori_loop(0, 4, factor_block, 0)

    pick = lax.broadcasted_iota(jnp.int32, (8, 512), 1) == me * 8 + lax.broadcasted_iota(jnp.int32, (8, 512), 0)
    factor_ref[...] = dot32(pick.astype(jnp.float32), lt[...], tb=True)
    own = zg[:, pl.ds(z, 1)].reshape(TILES * SLAB, WIDTH)
    wv = w[...]
    solved_ref[...] = dot48(own, wv, tb=True).reshape(TILES, SLAB, WIDTH)
    lt[...] = dot48(wv.T, wv)
    for t in range(TILES):
        bhi[t], blo[t] = split(dot48(zg[t].reshape(TW, WIDTH), lt[...]))

    for c in trail_in:
        c.start()
    for pos in (0, 1, 4, 2, 5, 3, 6, 7):
        yy = (y + step_of[pos]) % 8
        remote(sb.at[:, 0], sb.at[:, 0], sb_s, sb_r.at[pos], dev(dx=1)).wait_recv()
        back = (-step_of[pos]) % 8
        if back == 0:
            sa_copy(0).wait_recv()
        else:
            remote(pa.at[0], pa.at[0], sa_s, sa_r.at[back], dev(dy=1)).wait_recv()

        def convert(i, c, yy=yy):
            v = jnp.concatenate([pb[i // 2, i % 2, yy], pa[yy, i % 2, i // 2]], axis=0)
            hi, lo = split(v)
            at = (i // 2 * 8 + yy) * 2 + i % 2
            ph[at] = hi
            pll[at] = lo
            return c

        lax.fori_loop(0, 8, convert, 0)

    loads[7].wait()
    for t in range(TILES):
        live, hi, lo = [], [], []
        for s in range(SLOTS):
            p = slots_s[t, s, me]
            live.append((p >= 0).astype(jnp.float32))
            src = jnp.maximum(p, 0) // TILES
            hi.append(ph[src])
            lo.append(pll[src])
        hi, lo = jnp.concatenate(hi, axis=0), jnp.concatenate(lo, axis=0)
        bh, bl = bhi[t], blo[t]
        upd = dot16(hi, bh) + (dot16(hi, bl) + dot16(lo, bh))
        trail_in[t].wait()
        for s in range(SLOTS):
            out_v[t, s] = trail_v[t, s] - upd[s * SLAB : s * SLAB + SLAB] * live[s]
        trail_out[t].start()

    for c in range(4):

        @pl.when(x >= c)
        def _(c=c):
            dy_all(c).wait_send()
            dx_all(c).wait_send()

        dk_copy(c).wait_send()
    xa_all.wait_send()
    for step in range(4):
        for way in range(2):
            z_copy(step, way).wait_send()
            y_copy(step, way).wait_send()
    remote(sb, sb, sb_s, sb_r.at[0], dev(dx=1)).wait_send()
    remote(sa, sa, sa_s, sa_r.at[0], dev(dy=1)).wait_send()
    for c in trail_out:
        c.wait()


def deliver(factor_ref, solved_ref, trail_ref, factor_out, solved_out, trail_out, fv, sv, tv, i_sem, o_sem):
    stages = [(trail_ref.at[t], tv.at[t], trail_out.at[t]) for t in range(TILES)]
    stages += [(solved_ref, sv, solved_out), (factor_ref, fv, factor_out)]
    come = [pltpu.make_async_copy(a, b, i_sem.at[n]) for n, (a, b, _) in enumerate(stages)]
    leave = [pltpu.make_async_copy(b, c, o_sem.at[n]) for n, (_, b, c) in enumerate(stages)]
    for c in come:
        c.start()
    for a, b in zip(come, leave):
        a.wait()
        b.start()
    for c in leave:
        c.wait()


def per_device(diag_block, panel, panel_mask, slot_rows, trail):
    f32, i32 = jnp.float32, jnp.int32
    vm = lambda *shape: pltpu.VMEM(shape, f32)
    dma = lambda *shape: pltpu.SemaphoreType.DMA(shape)
    one = pltpu.SemaphoreType.DMA
    vmem = pl.BlockSpec(memory_space=pltpu.VMEM)
    hbm = pl.BlockSpec(memory_space=pl.ANY)
    shapes = (
        jax.ShapeDtypeStruct(diag_block.shape, f32),
        jax.ShapeDtypeStruct(panel.shape, f32),
        jax.ShapeDtypeStruct(trail.shape, f32),
    )
    slots = jnp.transpose(slot_rows, (1, 2, 0))
    bf = lambda *shape: pltpu.VMEM(shape, jnp.bfloat16)
    results = pl.pallas_call(
        kernel,
        out_shape=shapes,
        in_specs=[hbm] * 5,
        out_specs=(vmem, vmem, hbm),
        scratch_shapes=[
            vm(4, NK, NX, NY, 8, 128), vm(512, 512), vm(512, 512), vm(128, 128), vm(128, 128),
            vm(NX, TILES, RA, WIDTH), vm(TILES, NZ, SLAB, WIDTH),
            *[vm(TILES, RB, WIDTH) for _ in range(8)],
            vm(7, 8, RB, WIDTH), vm(15, NX, RA, WIDTH),
            vm(NX, NK, NY, RB, WIDTH), vm(NY, NK, NX, RA, WIDTH),
            bf(TILES, TW, WIDTH), bf(TILES, TW, WIDTH), bf(64, SLAB, WIDTH), bf(64, SLAB, WIDTH),
            vm(TILES, SLOTS, SLAB, TW), vm(TILES, SLOTS, SLAB, TW),
            vm(TILES, SLAB, WIDTH), pltpu.VMEM((2, TILES), i32), pltpu.VMEM(slots.shape, i32),
            pltpu.SMEM(slots.shape, i32), pltpu.VMEM((16, 64), i32), pltpu.SMEM((16, 64), i32),
            dma(4), dma(4), dma(4), dma(4, 3), dma(4), dma(4), one, one,
            dma(4, 2), dma(4, 2), dma(4, 2), dma(4, 2), one, dma(8), one, dma(8),
            dma(9), dma(4), dma(4),
        ],
        compiler_params=pltpu.CompilerParams(
            collective_id=0, has_side_effects=True, vmem_limit_bytes=58 * 1024 * 1024
        ),
        name="panels",
    )(diag_block, panel, panel_mask.T, slots, trail)
    return pl.pallas_call(
        deliver,
        out_shape=shapes,
        in_specs=[hbm] * 3,
        out_specs=(hbm,) * 3,
        scratch_shapes=[vm(*diag_block.shape), vm(*panel.shape), vm(*trail.shape), dma(6), dma(6)],
        compiler_params=pltpu.CompilerParams(vmem_limit_bytes=58 * 1024 * 1024),
        name="deliver",
    )(*results)


def solution(mesh):
    in_specs = (
        P("row", None),
        P("row", "col", None),
        P("row", None),
        P(),
        P("row", None, "col", None),
    )
    out_specs = (P("row", None), P("row", "col", None), P("row", None, "col", None))
    return jax.shard_map(
        per_device, mesh=mesh, in_specs=in_specs, out_specs=out_specs, check_vma=False
    )
```

```python
import jax
import jax.numpy as jnp
from jax import lax
from jax.experimental import pallas as pl
from jax.experimental.pallas import tpu as pltpu
from jax.sharding import PartitionSpec as P

MESH = pl.DeviceIdType.MESH
HI = lax.Precision.HIGHEST
NX, NY, NK, NZ = 4, 8, 2, 8
TILES, SLAB, WIDTH, TW = 4, 32, 512, 256
RB, RA = 24, 8
SLOTS = 16
SCHEDULE = {(0, 10): (("y", 1),), (0, 16): (("z", 1),), (1, 10): (("y", 2),), (1, 16): (("z", 2),), (2, 8): (("y", 3),), (2, 16): (("z", 3),)}
CUTS = (4, 8, 12, 15)


def dot32(a, b, tb=False):
    dims = (((1,), (1 if tb else 0,)), ((), ()))
    return lax.dot_general(a, b, dims, precision=HI, preferred_element_type=jnp.float32)


def dot16(a, b):
    dims = (((1,), (1,)), ((), ()))
    return lax.dot_general(a, b, dims, preferred_element_type=jnp.float32)


def split(x):
    hi = x.astype(jnp.bfloat16)
    lo = (x - hi.astype(jnp.float32)).astype(jnp.bfloat16)
    return hi, lo


def dot48(a, b, tb=False):
    dims = (((1,), (1 if tb else 0,)), ((), ()))
    ah, al = split(a)
    bh, bl = split(b)
    dot = lambda p, q: lax.dot_general(p, q, dims, preferred_element_type=jnp.float32)
    return dot(ah, bh) + (dot(ah, bl) + dot(al, bh))


def lanes(x, lane):
    return jnp.broadcast_to(x[:, lane : lane + 1], x.shape)


def rows(x, row):
    return jnp.broadcast_to(x[row : row + 1, :], (8, 128))


def total(xs):
    while len(xs) > 1:
        xs = [xs[i] + xs[i + 1] if i + 1 < len(xs) else xs[i] for i in range(0, len(xs), 2)]
    return xs[0]


def pivot8(cols):
    d, low, rs, inv = {}, {}, {}, {}
    for b in range(8):
        for a in range(b, 8):
            d[a, b] = rows(cols[b], a)
    for k in range(8):
        rs[k] = lax.rsqrt(d[k, k])
        for i in range(k + 1, 8):
            low[i, k] = d[i, k] * rs[k]
        for i in range(k + 1, 8):
            for j in range(k + 1, i + 1):
                d[i, j] = d[i, j] - low[i, k] * low[j, k]
        inv[k, k] = rs[k]
        for m in range(k):
            s = low[k, m] * inv[m, m]
            for q in range(m + 1, k):
                s = s + low[k, q] * inv[q, m]
            inv[k, m] = -(rs[k] * s)
    return inv


def sweep8(j, m_ref, lt_ref):
    r0 = j * 8
    sub = lax.broadcasted_iota(jnp.int32, (8, 128), 0)
    lane = lax.broadcasted_iota(jnp.int32, (8, 128), 1)
    block = m_ref[r0 : r0 + 8, :]
    inv = pivot8([lanes(block, r0 + b) for b in range(8)])
    zero = jnp.zeros((8, 128), jnp.float32)
    colv, rowv = [], []
    for m in range(8):
        v = zero
        for k in range(m, 8):
            v = jnp.where(sub == k, inv[k, m], v)
        colv.append(v)
    for k in range(8):
        v = zero
        for m in range(k + 1):
            v = jnp.where(sub == m, inv[k, m], v)
        rowv.append(v)
    inside = (lane >= r0) & (lane < r0 + 8)
    u = total([colv[m] * rows(block, m) for m in range(8)])
    lt_ref[r0 : r0 + 8, :] = jnp.where(lane >= r0 + sub, u, 0.0)
    pattern = zero
    for m in range(8):
        pattern = jnp.where(lane == r0 + m, colv[m], pattern)
    u = jnp.where(inside, pattern, u)
    p = total([rowv[k] * rows(u, k) for k in range(8)])
    spread = [rows(p, m) for m in range(8)]
    m_ref[r0 : r0 + 8, :] = u
    for i in range(j + 1, 16):
        mi = m_ref[8 * i : 8 * i + 8, :]
        upd = total([lanes(mi, r0 + m) * spread[m] for m in range(8)])
        m_ref[8 * i : 8 * i + 8, :] = jnp.where(inside, 0.0, mi) - upd


def block_update(J, a_ref, lt_ref, blk, ltb):
    r0, r1 = J * 128, J * 128 + 128
    tri = lax.broadcasted_iota(jnp.int32, (128, 128), 0) >= lax.broadcasted_iota(jnp.int32, (128, 128), 1)
    linv = jnp.where(tri, blk[...], 0.0)
    lt_ref[r0:r1, r0:r1] = ltb[...]
    if J > 0:
        uw = dot32(linv, a_ref[r0:r1, :r0])
        a_ref[r0:r1, :r0] = uw
    if J < 3:
        lcol = dot32(a_ref[r1:, r0:r1], linv, tb=True)
        ut = lcol.T
        lt_ref[r0:r1, r1:] = ut
        a_ref[r1:, r1:] = a_ref[r1:, r1:] - dot32(lcol, ut)
        a_ref[r1:, r0:r1] = -dot32(lcol, linv)
        if J > 0:
            a_ref[r1:, :r0] = a_ref[r1:, :r0] - dot32(lcol, uw)
    a_ref[r0:r1, r0:r1] = linv
    if J < 3:
        a_ref[r0:r1, r1:] = jnp.zeros((128, 512 - r1), jnp.float32)


def kernel(
    diag_ref, panel_ref, mask_ref, slots_ref, trail_ref,
    factor_ref, solved_ref, out_ref,
    a7, w, lt, blk, ltb, xa, zg, yb0, yb1, yb2, yb3, yb4, yb5, yb6, yb7,
    sb, sa, pb, pa, bhi, blo, ph, pll, trail_v, out_v, panel_v, mask_v, slots_v, slots_s, table_v, table_s,
    dy_s, dy_r, dx_s, dx_r, dk_s, dk_r, xa_s, xa_r, z_s, z_r, y_s, y_r, sb_s, sb_r, sa_s, sa_r, l_sem, t_sem, o_sem,
):
    me = lax.axis_index("row")
    z = lax.axis_index("col")
    x, y, k = me // 16, (me // 2) % 8, me % 2

    def dev(dx=0, dy=0, dk=0, dz=0):
        return (((x + dx) % 4 * 8 + (y + dy) % 8) * 2 + (k + dk) % 2, (z + dz) % 8)

    def remote(src, dst, ss, rs, to):
        return pltpu.make_async_remote_copy(src, dst, ss, rs, device_id=to, device_id_type=MESH)

    loads = [
        pltpu.make_async_copy(diag_ref.at[:, pl.ds(c * 128, 128)], a7.at[c, k, x, y], l_sem.at[c])
        for c in range(4)
    ]
    loads += [
        pltpu.make_async_copy(panel_ref, panel_v, l_sem.at[4]),
        pltpu.make_async_copy(mask_ref, mask_v, l_sem.at[5]),
        pltpu.make_async_copy(slots_ref, slots_v, l_sem.at[6]),
        pltpu.make_async_copy(slots_ref, slots_s, l_sem.at[8]),
    ]
    for c in loads:
        c.start()
    trail_in = [pltpu.make_async_copy(trail_ref.at[t], trail_v.at[t], t_sem.at[t]) for t in range(TILES)]
    trail_out = [pltpu.make_async_copy(out_v.at[t], out_ref.at[t], o_sem.at[t]) for t in range(TILES)]

    barrier = pltpu.get_barrier_semaphore()
    partners = [dev(dz=1), dev(dz=-1)]
    partners += [dev(dx=e // 2, dk=e % 2) for e in range(1, 8)]
    partners += [dev(dy=e // 2, dk=e % 2) for e in range(2, 16)]
    for to in partners:
        pl.semaphore_signal(barrier, inc=1, device_id=to, device_id_type=MESH)
    for c in loads[:6]:
        c.wait()

    first_half = lax.broadcasted_iota(jnp.int32, (SLAB, WIDTH), 1) < TW
    mask = mask_v[...].astype(jnp.float32)
    for t in range(TILES):
        keep = jnp.where(
            first_half,
            jnp.broadcast_to(mask[0:1, t : t + 1], (SLAB, WIDTH)),
            jnp.broadcast_to(mask[1:2, t : t + 1], (SLAB, WIDTH)),
        )
        v = panel_v[t] * keep
        zg[t, pl.ds(z, 1)] = v[None]
        yb0[t] = v[:RB]
        xa[pl.ds(x, 1), t] = v[RB:][None]
    pl.semaphore_wait(barrier, len(partners))

    def dy_copy(c, i):
        ref = a7.at[c, k, x, y]
        return remote(ref, ref, dy_s.at[c], dy_r.at[c], dev(dy=i + 1))

    def dx_copy(c, i):
        ref = a7.at[c, k, x]
        return remote(ref, ref, dx_s.at[c], dx_r.at[c, i], dev(dx=i + 1))

    def dy_all(c):
        ref = a7.at[c, k, x, pl.ds(0, 7)]
        return remote(ref, ref, dy_s.at[c], dy_r.at[c], dev(dy=1))

    def dx_all(c):
        ref = a7.at[c, k, pl.ds(0, 3)]
        return remote(ref, ref, dx_s.at[c], dx_r.at[c, 0], dev(dx=1))

    def dk_copy(c):
        ref = a7.at[c, k, pl.ds(c, 4 - c)]
        return remote(ref, ref, dk_s.at[c], dk_r.at[c], dev(dk=1))

    def start_dy(c):
        @pl.when(x >= c)
        def _():
            for i in range(7):
                dy_copy(c, i).start()

    start_dy(0)

    yb = [yb0, yb1, yb2, yb3, yb4, yb5, yb6, yb7]
    step_of = {0: 0, 1: -1, 2: -2, 3: -3, 4: 1, 5: 2, 6: 3, 7: 4}

    def ring(step, way):
        src = 0 if step == 0 else (step if way == 0 else step + 3)
        dst = 7 if step == 3 else (step + 1 if way == 0 else step + 4)
        part = pl.ds(0, TILES) if step < 3 else pl.ds(2 * way, 2)
        return src, dst, part

    def z_copy(step, way):
        src, _, part = ring(step, way)
        block = (z + step_of[src]) % 8
        ref = zg.at[part, block]
        return remote(ref, ref, z_s.at[step, way], z_r.at[step, way], dev(dz=1 if way == 0 else -1))

    def y_copy(step, way):
        src, dst, part = ring(step, way)
        return remote(
            yb[src].at[part], yb[dst].at[part], y_s.at[step, way], y_r.at[step, way],
            dev(dy=1 if way == 0 else -1),
        )

    def xa_copy(i):
        return remote(xa.at[x], xa.at[x], xa_s, xa_r, dev(dx=i + 1))

    xa_all = remote(xa.at[pl.ds(0, 3)], xa.at[pl.ds(0, 3)], xa_s, xa_r, dev(dx=1))
    for way in range(2):
        y_copy(0, way).start()
    for c in range(1, 4):
        start_dy(c)
    for i in range(3):
        xa_copy(i).start()
    for way in range(2):
        z_copy(0, way).start()

    loads[6].wait()
    wanted = slots_v[...].reshape(TILES * SLOTS, 64)
    source_row, tile = wanted >> 2, wanted & 3
    sub16 = lax.broadcasted_iota(jnp.int32, (16, 64), 0)
    table = jnp.zeros((16, 64), jnp.int32)
    for i in range(12):
        src = (x * 8 + i) * 2 + k if i < 8 else ((i - 8) * 8 + y) * 2 + k
        best = jnp.max(jnp.where(source_row == src, tile, 0), axis=0, keepdims=True)
        table = jnp.where(sub16 == i, best, table)
    table_v[...] = table
    to_scalar = pltpu.make_async_copy(table_v, table_s, l_sem.at[7])
    to_scalar.start()

    def sb_copy(pos, e, yy):
        return remote(
            sb.at[e, pos], pb.at[x, k, yy], sb_s, sb_r.at[pos],
            dev(dx=(e + 1) // 2, dk=(e + 1) % 2),
        )

    def send_block(pos):
        yy = (y + step_of[pos]) % 8
        buf = yb[pos]
        pb[x, k, yy] = buf[table_s[yy, me]]

        def body(e, c):
            to = dev(dx=(e + 1) // 2, dk=(e + 1) % 2)[0]
            sb[e, pos] = buf[table_s[yy, to]]
            sb_copy(pos, e, yy).start()
            return c

        lax.fori_loop(0, 7, body, 0)

    def sa_to(e):
        m = (e + 1) // 2
        d = (m + 1) // 2
        return (8 + d * (2 * (m % 2) - 1)) % 8, (e + 1) % 2

    def sa_copy(e):
        dy, dk = sa_to(e)
        return remote(sa.at[e], pa.at[y, k], sa_s, sa_r.at[dy], dev(dy=dy, dk=dk))

    def send_cross(lo, hi):
        def body(e, c):
            dy, dk = sa_to(e)
            to = dev(dy=dy, dk=dk)[0]
            for xx in range(NX):
                sa[e, xx] = xa[xx, table_s[8 + xx, to]]
            sa_copy(e).start()
            return c

        lax.fori_loop(lo, hi, body, 0)

    def service_y(step):
        for way in range(2):
            y_copy(step, way).wait_recv()
            if step < 3:
                y_copy(step + 1, way).start()
        if step < 3:
            send_block(step + 1)
            send_block(step + 4)
        else:
            send_block(7)

    def service_z(step):
        for way in range(2):
            z_copy(step, way).wait_recv()
            if step < 3:
                z_copy(step + 1, way).start()

    def turn_diag(c):
        @pl.when(x >= c)
        def _():
            dy_all(c).wait_recv()
            for i in range(3):
                dx_copy(c, i).start()

    def pass_diag(c):
        for i in range(3):

            @pl.when((x + 3 - i) % 4 >= c)
            def _(i=i):
                dx_copy(c, i).wait_recv()

        dk_copy(c).start()

    def unpack(c):
        dk_copy(c).wait_recv()
        for xx in range(c, NX):
            v = jnp.stack([a7[c, 0, xx], a7[c, 1, xx]], axis=1)
            w[xx * 128 : xx * 128 + 128, c * 128 : c * 128 + 128] = v.reshape(128, 128)

    to_scalar.wait()
    send_block(0)
    turn_diag(0)
    xa_all.wait_recv()
    for c in range(1, 4):
        turn_diag(c)
    for xx in range(NX):
        pa[y, k, xx] = xa[xx, table_s[8 + xx, me]]
    w[...] = jnp.zeros_like(w)
    lt[...] = jnp.zeros_like(lt)
    service_y(0)
    send_cross(0, CUTS[0])
    pass_diag(0)
    service_z(0)
    unpack(0)

    def serve(what):
        for axis, step in what:
            if axis == "y":
                service_y(step)
                send_cross(CUTS[step - 1], CUTS[step])
            else:
                service_z(step)

    def factor_block(J, carry):
        r0 = pl.multiple_of(J * 128, 128)
        blk[...] = w[pl.ds(r0, 128), pl.ds(r0, 128)]
        for j in range(16):
            if j == 5:

                @pl.when(J == 0)
                def _():
                    for c in range(1, 4):
                        pass_diag(c)

            for s in range(4):
                if (s, j) in SCHEDULE:

                    @pl.when(J == s)
                    def _(s=s, j=j):
                        serve(SCHEDULE[s, j])

            sweep8(j, blk, ltb)
        for s in range(4):

            @pl.when(J == s)
            def _(s=s):
                if s == 0:
                    for c in range(1, 4):
                        unpack(c)
                block_update(s, w, lt, blk, ltb)
                serve(SCHEDULE.get((s, 16), ()))

        return carry

    lax.fori_loop(0, 4, factor_block, 0)

    pick = lax.broadcasted_iota(jnp.int32, (8, 512), 1) == me * 8 + lax.broadcasted_iota(jnp.int32, (8, 512), 0)
    factor_ref[...] = dot32(pick.astype(jnp.float32), lt[...], tb=True)
    own = zg[:, pl.ds(z, 1)].reshape(TILES * SLAB, WIDTH)
    wv = w[...]
    solved_ref[...] = dot48(own, wv, tb=True).reshape(TILES, SLAB, WIDTH)
    lt[...] = dot48(wv.T, wv)
    for t in range(TILES):
        bhi[t], blo[t] = split(dot48(zg[t].reshape(TW, WIDTH), lt[...]))

    for c in trail_in:
        c.start()
    for pos in (0, 1, 4, 2, 5, 3, 6, 7):
        yy = (y + step_of[pos]) % 8
        remote(sb.at[:, 0], sb.at[:, 0], sb_s, sb_r.at[pos], dev(dx=1)).wait_recv()
        back = (-step_of[pos]) % 8
        if back == 0:
            sa_copy(0).wait_recv()
        else:
            remote(pa.at[0], pa.at[0], sa_s, sa_r.at[back], dev(dy=1)).wait_recv()

        def convert(i, c, yy=yy):
            v = jnp.concatenate([pb[i // 2, i % 2, yy], pa[yy, i % 2, i // 2]], axis=0)
            hi, lo = split(v)
            at = (i // 2 * 8 + yy) * 2 + i % 2
            ph[at] = hi
            pll[at] = lo
            return c

        lax.fori_loop(0, 8, convert, 0)

    loads[7].wait()
    for t in range(TILES):
        live, hi, lo = [], [], []
        for s in range(SLOTS):
            p = slots_s[t, s, me]
            live.append((p >= 0).astype(jnp.float32))
            src = jnp.maximum(p, 0) // TILES
            hi.append(ph[src])
            lo.append(pll[src])
        hi, lo = jnp.concatenate(hi, axis=0), jnp.concatenate(lo, axis=0)
        bh, bl = bhi[t], blo[t]
        upd = dot16(hi, bh) + (dot16(hi, bl) + dot16(lo, bh))
        trail_in[t].wait()
        for s in range(SLOTS):
            out_v[t, s] = trail_v[t, s] - upd[s * SLAB : s * SLAB + SLAB] * live[s]
        trail_out[t].start()

    for c in range(4):

        @pl.when(x >= c)
        def _(c=c):
            dy_all(c).wait_send()
            dx_all(c).wait_send()

        dk_copy(c).wait_send()
    xa_all.wait_send()
    for step in range(4):
        for way in range(2):
            z_copy(step, way).wait_send()
            y_copy(step, way).wait_send()
    remote(sb, sb, sb_s, sb_r.at[0], dev(dx=1)).wait_send()
    remote(sa, sa, sa_s, sa_r.at[0], dev(dy=1)).wait_send()
    for c in trail_out:
        c.wait()


def deliver(factor_ref, solved_ref, trail_ref, factor_out, solved_out, trail_out, fv, sv, tv, i_sem, o_sem):
    stages = [(trail_ref.at[t], tv.at[t], trail_out.at[t]) for t in range(TILES)]
    stages += [(solved_ref, sv, solved_out), (factor_ref, fv, factor_out)]
    come = [pltpu.make_async_copy(a, b, i_sem.at[n]) for n, (a, b, _) in enumerate(stages)]
    leave = [pltpu.make_async_copy(b, c, o_sem.at[n]) for n, (_, b, c) in enumerate(stages)]
    for c in come:
        c.start()
    for a, b in zip(come, leave):
        a.wait()
        b.start()
    for c in leave:
        c.wait()


def per_device(diag_block, panel, panel_mask, slot_rows, trail):
    f32, i32 = jnp.float32, jnp.int32
    vm = lambda *shape: pltpu.VMEM(shape, f32)
    dma = lambda *shape: pltpu.SemaphoreType.DMA(shape)
    one = pltpu.SemaphoreType.DMA
    vmem = pl.BlockSpec(memory_space=pltpu.VMEM)
    hbm = pl.BlockSpec(memory_space=pl.ANY)
    shapes = (
        jax.ShapeDtypeStruct(diag_block.shape, f32),
        jax.ShapeDtypeStruct(panel.shape, f32),
        jax.ShapeDtypeStruct(trail.shape, f32),
    )
    slots = jnp.transpose(slot_rows, (1, 2, 0))
    bf = lambda *shape: pltpu.VMEM(shape, jnp.bfloat16)
    results = pl.pallas_call(
        kernel,
        out_shape=shapes,
        in_specs=[hbm] * 5,
        out_specs=(vmem, vmem, hbm),
        scratch_shapes=[
            vm(4, NK, NX, NY, 8, 128), vm(512, 512), vm(512, 512), vm(128, 128), vm(128, 128),
            vm(NX, TILES, RA, WIDTH), vm(TILES, NZ, SLAB, WIDTH),
            *[vm(TILES, RB, WIDTH) for _ in range(8)],
            vm(7, 8, RB, WIDTH), vm(15, NX, RA, WIDTH),
            vm(NX, NK, NY, RB, WIDTH), vm(NY, NK, NX, RA, WIDTH),
            bf(TILES, TW, WIDTH), bf(TILES, TW, WIDTH), bf(64, SLAB, WIDTH), bf(64, SLAB, WIDTH),
            vm(TILES, SLOTS, SLAB, TW), vm(TILES, SLOTS, SLAB, TW),
            vm(TILES, SLAB, WIDTH), pltpu.VMEM((2, TILES), i32), pltpu.VMEM(slots.shape, i32),
            pltpu.SMEM(slots.shape, i32), pltpu.VMEM((16, 64), i32), pltpu.SMEM((16, 64), i32),
            dma(4), dma(4), dma(4), dma(4, 3), dma(4), dma(4), one, one,
            dma(4, 2), dma(4, 2), dma(4, 2), dma(4, 2), one, dma(8), one, dma(8),
            dma(9), dma(4), dma(4),
        ],
        compiler_params=pltpu.CompilerParams(
            collective_id=0, has_side_effects=True, vmem_limit_bytes=58 * 1024 * 1024
        ),
        name="panels",
    )(diag_block, panel, panel_mask.T, slots, trail)
    return pl.pallas_call(
        deliver,
        out_shape=shapes,
        in_specs=[hbm] * 3,
        out_specs=(hbm,) * 3,
        scratch_shapes=[vm(*diag_block.shape), vm(*panel.shape), vm(*trail.shape), dma(6), dma(6)],
        compiler_params=pltpu.CompilerParams(vmem_limit_bytes=58 * 1024 * 1024),
        name="deliver",
    )(*results)


def solution(mesh):
    in_specs = (
        P("row", None),
        P("row", "col", None),
        P("row", None),
        P(),
        P("row", None, "col", None),
    )
    out_specs = (P("row", None), P("row", "col", None), P("row", None, "col", None))
    return jax.shard_map(
        per_device, mesh=mesh, in_specs=in_specs, out_specs=out_specs, check_vma=False
    )
```

```python
import jax
import jax.numpy as jnp
from jax import lax
from jax.experimental import pallas as pl
from jax.experimental.pallas import tpu as pltpu
from jax.sharding import PartitionSpec as P

MESH = pl.DeviceIdType.MESH
HI = lax.Precision.HIGHEST
NX, NY, NK, NZ = 4, 8, 2, 8
TILES, SLAB, WIDTH, TW = 4, 32, 512, 256
RB, RA = 24, 8
SLOTS = 16
SCHEDULE = {(0, 10): (("y", 1),), (0, 16): (("z", 1),), (1, 10): (("y", 2),), (1, 16): (("z", 2),), (2, 8): (("y", 3),), (2, 16): (("z", 3),)}
CUTS = (4, 8, 12, 15)


def dot32(a, b, tb=False):
    dims = (((1,), (1 if tb else 0,)), ((), ()))
    return lax.dot_general(a, b, dims, precision=HI, preferred_element_type=jnp.float32)


def dot16(a, b):
    dims = (((1,), (1,)), ((), ()))
    return lax.dot_general(a, b, dims, preferred_element_type=jnp.float32)


def dot_nn(a, b):
    return lax.dot_general(a, b, (((1,), (0,)), ((), ())), preferred_element_type=jnp.float32)


def split(x):
    hi = x.astype(jnp.bfloat16)
    lo = (x - hi.astype(jnp.float32)).astype(jnp.bfloat16)
    return hi, lo


def dot48(a, b, tb=False):
    dims = (((1,), (1 if tb else 0,)), ((), ()))
    ah, al = split(a)
    bh, bl = split(b)
    dot = lambda p, q: lax.dot_general(p, q, dims, preferred_element_type=jnp.float32)
    return dot(ah, bh) + (dot(ah, bl) + dot(al, bh))


def lanes(x, lane):
    return jnp.broadcast_to(x[:, lane : lane + 1], x.shape)


def rows(x, row):
    return jnp.broadcast_to(x[row : row + 1, :], (8, 128))


def total(xs):
    while len(xs) > 1:
        xs = [xs[i] + xs[i + 1] if i + 1 < len(xs) else xs[i] for i in range(0, len(xs), 2)]
    return xs[0]


def pivot8(cols):
    d, low, rs, inv = {}, {}, {}, {}
    for b in range(8):
        for a in range(b, 8):
            d[a, b] = rows(cols[b], a)
    for k in range(8):
        rs[k] = lax.rsqrt(d[k, k])
        for i in range(k + 1, 8):
            low[i, k] = d[i, k] * rs[k]
        for i in range(k + 1, 8):
            for j in range(k + 1, i + 1):
                d[i, j] = d[i, j] - low[i, k] * low[j, k]
        inv[k, k] = rs[k]
        for m in range(k):
            s = low[k, m] * inv[m, m]
            for q in range(m + 1, k):
                s = s + low[k, q] * inv[q, m]
            inv[k, m] = -(rs[k] * s)
    return inv


def sweep8(j, m_ref, lt_ref):
    r0 = j * 8
    sub = lax.broadcasted_iota(jnp.int32, (8, 128), 0)
    lane = lax.broadcasted_iota(jnp.int32, (8, 128), 1)
    block = m_ref[r0 : r0 + 8, :]
    inv = pivot8([lanes(block, r0 + b) for b in range(8)])
    zero = jnp.zeros((8, 128), jnp.float32)
    colv, rowv = [], []
    for m in range(8):
        v = zero
        for k in range(m, 8):
            v = jnp.where(sub == k, inv[k, m], v)
        colv.append(v)
    for k in range(8):
        v = zero
        for m in range(k + 1):
            v = jnp.where(sub == m, inv[k, m], v)
        rowv.append(v)
    inside = (lane >= r0) & (lane < r0 + 8)
    u = total([colv[m] * rows(block, m) for m in range(8)])
    lt_ref[r0 : r0 + 8, :] = jnp.where(lane >= r0 + sub, u, 0.0)
    pattern = zero
    for m in range(8):
        pattern = jnp.where(lane == r0 + m, colv[m], pattern)
    u = jnp.where(inside, pattern, u)
    p = total([rowv[k] * rows(u, k) for k in range(8)])
    spread = [rows(p, m) for m in range(8)]
    m_ref[r0 : r0 + 8, :] = u
    for i in range(j + 1, 16):
        mi = m_ref[8 * i : 8 * i + 8, :]
        upd = total([lanes(mi, r0 + m) * spread[m] for m in range(8)])
        m_ref[8 * i : 8 * i + 8, :] = jnp.where(inside, 0.0, mi) - upd


def block_update(J, a_ref, lt_ref, blk, ltb):
    r0, r1 = J * 128, J * 128 + 128
    tri = lax.broadcasted_iota(jnp.int32, (128, 128), 0) >= lax.broadcasted_iota(jnp.int32, (128, 128), 1)
    linv = jnp.where(tri, blk[...], 0.0)
    lt_ref[r0:r1, r0:r1] = ltb[...]
    if J > 0:
        uw = dot32(linv, a_ref[r0:r1, :r0])
        a_ref[r0:r1, :r0] = uw
    if J < 3:
        lcol = dot32(a_ref[r1:, r0:r1], linv, tb=True)
        ut = lcol.T
        lt_ref[r0:r1, r1:] = ut
        a_ref[r1:, r1:] = a_ref[r1:, r1:] - dot32(lcol, ut)
        a_ref[r1:, r0:r1] = -dot32(lcol, linv)
        if J > 0:
            a_ref[r1:, :r0] = a_ref[r1:, :r0] - dot32(lcol, uw)
    a_ref[r0:r1, r0:r1] = linv
    if J < 3:
        a_ref[r0:r1, r1:] = jnp.zeros((128, 512 - r1), jnp.float32)


def kernel(
    diag_ref, panel_ref, mask_ref, slots_ref, trail_ref,
    factor_ref, solved_ref, out_ref,
    a7, w, lt, blk, ltb, turn, avh, avl, xa, zg, yb0, yb1, yb2, yb3, yb4, yb5, yb6, yb7,
    sb, sa, pb, pa, bhi, blo, ph, pll, trail_v, out_v, panel_v, mask_v, slots_v, slots_s, table_v, table_s,
    dy_s, dy_r, dx_s, dx_r, dk_s, dk_r, xa_s, xa_r, z_s, z_r, y_s, y_r, sb_s, sb_r, sa_s, sa_r, l_sem, t_sem, o_sem,
):
    me = lax.axis_index("row")
    z = lax.axis_index("col")
    x, y, k = me // 16, (me // 2) % 8, me % 2

    def dev(dx=0, dy=0, dk=0, dz=0):
        return (((x + dx) % 4 * 8 + (y + dy) % 8) * 2 + (k + dk) % 2, (z + dz) % 8)

    def remote(src, dst, ss, rs, to):
        return pltpu.make_async_remote_copy(src, dst, ss, rs, device_id=to, device_id_type=MESH)

    loads = [
        pltpu.make_async_copy(diag_ref.at[:, pl.ds(c * 128, 128)], a7.at[c, k, x, y], l_sem.at[c])
        for c in range(4)
    ]
    loads += [
        pltpu.make_async_copy(panel_ref, panel_v, l_sem.at[4]),
        pltpu.make_async_copy(mask_ref, mask_v, l_sem.at[5]),
        pltpu.make_async_copy(slots_ref, slots_v, l_sem.at[6]),
        pltpu.make_async_copy(slots_ref, slots_s, l_sem.at[8]),
    ]
    for c in loads:
        c.start()
    trail_in = [pltpu.make_async_copy(trail_ref.at[t], trail_v.at[t], t_sem.at[t]) for t in range(TILES)]
    trail_out = [pltpu.make_async_copy(out_v.at[t], out_ref.at[t], o_sem.at[t]) for t in range(TILES)]

    barrier = pltpu.get_barrier_semaphore()
    partners = [dev(dz=1), dev(dz=-1)]
    partners += [dev(dx=e // 2, dk=e % 2) for e in range(1, 8)]
    partners += [dev(dy=e // 2, dk=e % 2) for e in range(2, 16)]
    for to in partners:
        pl.semaphore_signal(barrier, inc=1, device_id=to, device_id_type=MESH)
    for c in loads[:6]:
        c.wait()

    first_half = lax.broadcasted_iota(jnp.int32, (SLAB, WIDTH), 1) < TW
    mask = mask_v[...].astype(jnp.float32)
    for t in range(TILES):
        keep = jnp.where(
            first_half,
            jnp.broadcast_to(mask[0:1, t : t + 1], (SLAB, WIDTH)),
            jnp.broadcast_to(mask[1:2, t : t + 1], (SLAB, WIDTH)),
        )
        v = panel_v[t] * keep
        zg[t, pl.ds(z, 1)] = v[None]
        yb0[t] = v[:RB]
        xa[pl.ds(x, 1), t] = v[RB:][None]
    pl.semaphore_wait(barrier, len(partners))

    def dy_copy(c, i):
        ref = a7.at[c, k, x, y]
        return remote(ref, ref, dy_s.at[c], dy_r.at[c], dev(dy=i + 1))

    def dx_copy(c, i):
        ref = a7.at[c, k, x]
        return remote(ref, ref, dx_s.at[c], dx_r.at[c, i], dev(dx=i + 1))

    def dy_all(c):
        ref = a7.at[c, k, x, pl.ds(0, 7)]
        return remote(ref, ref, dy_s.at[c], dy_r.at[c], dev(dy=1))

    def dx_all(c):
        ref = a7.at[c, k, pl.ds(0, 3)]
        return remote(ref, ref, dx_s.at[c], dx_r.at[c, 0], dev(dx=1))

    def dk_copy(c):
        ref = a7.at[c, k, pl.ds(c, 4 - c)]
        return remote(ref, ref, dk_s.at[c], dk_r.at[c], dev(dk=1))

    def start_dy(c):
        @pl.when(x >= c)
        def _():
            for i in range(7):
                dy_copy(c, i).start()

    start_dy(0)

    yb = [yb0, yb1, yb2, yb3, yb4, yb5, yb6, yb7]
    step_of = {0: 0, 1: -1, 2: -2, 3: -3, 4: 1, 5: 2, 6: 3, 7: 4}

    def ring(step, way):
        src = 0 if step == 0 else (step if way == 0 else step + 3)
        dst = 7 if step == 3 else (step + 1 if way == 0 else step + 4)
        part = pl.ds(0, TILES) if step < 3 else pl.ds(2 * way, 2)
        return src, dst, part

    def z_copy(step, way):
        src, _, part = ring(step, way)
        block = (z + step_of[src]) % 8
        ref = zg.at[part, block]
        return remote(ref, ref, z_s.at[step, way], z_r.at[step, way], dev(dz=1 if way == 0 else -1))

    def y_copy(step, way):
        src, dst, part = ring(step, way)
        return remote(
            yb[src].at[part], yb[dst].at[part], y_s.at[step, way], y_r.at[step, way],
            dev(dy=1 if way == 0 else -1),
        )

    def xa_copy(i):
        return remote(xa.at[x], xa.at[x], xa_s, xa_r, dev(dx=i + 1))

    xa_all = remote(xa.at[pl.ds(0, 3)], xa.at[pl.ds(0, 3)], xa_s, xa_r, dev(dx=1))
    for way in range(2):
        y_copy(0, way).start()
    for c in range(1, 4):
        start_dy(c)
    for i in range(3):
        xa_copy(i).start()
    for way in range(2):
        z_copy(0, way).start()

    loads[6].wait()
    wanted = slots_v[...].reshape(TILES * SLOTS, 64)
    source_row, tile = wanted >> 2, wanted & 3
    sub16 = lax.broadcasted_iota(jnp.int32, (16, 64), 0)
    table = jnp.zeros((16, 64), jnp.int32)
    for i in range(12):
        src = (x * 8 + i) * 2 + k if i < 8 else ((i - 8) * 8 + y) * 2 + k
        best = jnp.max(jnp.where(source_row == src, tile, 0), axis=0, keepdims=True)
        table = jnp.where(sub16 == i, best, table)
    table_v[...] = table
    to_scalar = pltpu.make_async_copy(table_v, table_s, l_sem.at[7])
    to_scalar.start()

    def sb_copy(pos, e, yy):
        return remote(
            sb.at[e, pos], pb.at[x, k, yy], sb_s, sb_r.at[pos],
            dev(dx=(e + 1) // 2, dk=(e + 1) % 2),
        )

    def send_block(pos):
        yy = (y + step_of[pos]) % 8
        buf = yb[pos]
        pb[x, k, yy] = buf[table_s[yy, me]]

        def body(i, c):
            e = (i + 3) % 7
            to = dev(dx=(e + 1) // 2, dk=(e + 1) % 2)[0]
            sb[e, pos] = buf[table_s[yy, to]]
            sb_copy(pos, e, yy).start()
            return c

        lax.fori_loop(0, 7, body, 0)

    def sa_to(e):
        m = (e + 1) // 2
        d = (m + 1) // 2
        return (8 + d * (2 * (m % 2) - 1)) % 8, (e + 1) % 2

    def sa_copy(e):
        dy, dk = sa_to(e)
        return remote(sa.at[e], pa.at[y, k], sa_s, sa_r.at[dy], dev(dy=dy, dk=dk))

    def send_cross(lo, hi):
        def body(e, c):
            dy, dk = sa_to(e)
            to = dev(dy=dy, dk=dk)[0]
            for xx in range(NX):
                sa[e, xx] = xa[xx, table_s[8 + xx, to]]
            sa_copy(e).start()
            return c

        lax.fori_loop(lo, hi, body, 0)

    def service_y(step):
        for way in range(2):
            y_copy(step, way).wait_recv()
            if step < 3:
                y_copy(step + 1, way).start()
        if step < 3:
            send_block(step + 1)
            send_block(step + 4)
        else:
            send_block(7)

    def service_z(step):
        for way in range(2):
            z_copy(step, way).wait_recv()
            if step < 3:
                z_copy(step + 1, way).start()

    def turn_diag(c):
        @pl.when(x >= c)
        def _():
            dy_all(c).wait_recv()
            for i in range(3):
                dx_copy(c, i).start()

    def pass_diag(c):
        for i in range(3):

            @pl.when((x + 3 - i) % 4 >= c)
            def _(i=i):
                dx_copy(c, i).wait_recv()

        dk_copy(c).start()

    def unpack(c):
        dk_copy(c).wait_recv()
        for xx in range(c, NX):
            v = jnp.stack([a7[c, 0, xx], a7[c, 1, xx]], axis=1)
            w[xx * 128 : xx * 128 + 128, c * 128 : c * 128 + 128] = v.reshape(128, 128)

    to_scalar.wait()
    send_block(0)
    turn_diag(0)
    xa_all.wait_recv()
    for c in range(1, 4):
        turn_diag(c)
    for xx in range(NX):
        pa[y, k, xx] = xa[xx, table_s[8 + xx, me]]
    w[...] = jnp.zeros_like(w)
    lt[...] = jnp.zeros_like(lt)
    service_y(0)
    send_cross(0, CUTS[0])
    service_z(0)
    pass_diag(0)
    unpack(0)

    def serve(what):
        for axis, step in what:
            if axis == "y":
                service_y(step)
                send_cross(CUTS[step - 1], CUTS[step])
            else:
                service_z(step)

    def factor_block(J, carry):
        r0 = pl.multiple_of(J * 128, 128)
        blk[...] = w[pl.ds(r0, 128), pl.ds(r0, 128)]
        for j in range(16):
            if j == 5:

                @pl.when(J == 0)
                def _():
                    for c in range(1, 4):
                        pass_diag(c)

            for s in range(4):
                if (s, j) in SCHEDULE:

                    @pl.when(J == s)
                    def _(s=s, j=j):
                        serve(SCHEDULE[s, j])

            sweep8(j, blk, ltb)
        for s in range(4):

            @pl.when(J == s)
            def _(s=s):
                if s == 0:
                    for c in range(1, 4):
                        unpack(c)
                block_update(s, w, lt, blk, ltb)
                serve(SCHEDULE.get((s, 16), ()))

        return carry

    lax.fori_loop(0, 4, factor_block, 0)

    wv = w[...]
    wh, wl = split(wv)
    th, tl = split(wv.T)
    ainv = dot_nn(th, wh) + (dot_nn(th, wl) + dot_nn(tl, wh))
    avh[...], avl[...] = split(ainv)
    for t in range(TILES):
        qh, ql = split(zg[t].reshape(TW, WIDTH))
        bhi[t], blo[t] = split(dot_nn(qh, avh[...]) + (dot_nn(qh, avl[...]) + dot_nn(ql, avh[...])))

    turn[...] = lt[:, pl.ds(pl.multiple_of(me // 16 * 128, 128), 128)].T
    factor_ref[...] = turn[pl.ds(pl.multiple_of(me % 16 * 8, 8), 8), :]
    own = zg[:, pl.ds(z, 1)].reshape(TILES * SLAB, WIDTH)
    solved_ref[...] = dot48(own, w[...], tb=True).reshape(TILES, SLAB, WIDTH)

    for c in trail_in:
        c.start()
    for pos in (0, 1, 4, 2, 5, 3, 6, 7):
        yy = (y + step_of[pos]) % 8
        remote(sb.at[:, 0], sb.at[:, 0], sb_s, sb_r.at[pos], dev(dx=1)).wait_recv()
        back = (-step_of[pos]) % 8
        if back == 0:
            sa_copy(0).wait_recv()
        else:
            remote(pa.at[0], pa.at[0], sa_s, sa_r.at[back], dev(dy=1)).wait_recv()

        def convert(i, c, yy=yy):
            v = jnp.concatenate([pb[i // 2, i % 2, yy], pa[yy, i % 2, i // 2]], axis=0)
            hi, lo = split(v)
            at = (i // 2 * 8 + yy) * 2 + i % 2
            ph[at] = hi
            pll[at] = lo
            return c

        lax.fori_loop(0, 8, convert, 0)

    loads[7].wait()
    for t in range(TILES):
        live, hi, lo = [], [], []
        for s in range(SLOTS):
            p = slots_s[t, s, me]
            live.append((p >= 0).astype(jnp.float32))
            src = jnp.maximum(p, 0) // TILES
            hi.append(ph[src])
            lo.append(pll[src])
        hi, lo = jnp.concatenate(hi, axis=0), jnp.concatenate(lo, axis=0)
        bh, bl = bhi[t], blo[t]
        upd = dot16(hi, bh) + (dot16(hi, bl) + dot16(lo, bh))
        trail_in[t].wait()
        for s in range(SLOTS):
            out_v[t, s] = trail_v[t, s] - upd[s * SLAB : s * SLAB + SLAB] * live[s]
        trail_out[t].start()

    for c in range(4):

        @pl.when(x >= c)
        def _(c=c):
            dy_all(c).wait_send()
            dx_all(c).wait_send()

        dk_copy(c).wait_send()
    xa_all.wait_send()
    for step in range(4):
        for way in range(2):
            z_copy(step, way).wait_send()
            y_copy(step, way).wait_send()
    remote(sb, sb, sb_s, sb_r.at[0], dev(dx=1)).wait_send()
    remote(sa, sa, sa_s, sa_r.at[0], dev(dy=1)).wait_send()
    for c in trail_out:
        c.wait()


def deliver(factor_ref, solved_ref, trail_ref, factor_out, solved_out, trail_out, fv, sv, tv, i_sem, o_sem):
    stages = [(trail_ref.at[t], tv.at[t], trail_out.at[t]) for t in range(TILES)]
    stages += [(solved_ref, sv, solved_out), (factor_ref, fv, factor_out)]
    come = [pltpu.make_async_copy(a, b, i_sem.at[n]) for n, (a, b, _) in enumerate(stages)]
    leave = [pltpu.make_async_copy(b, c, o_sem.at[n]) for n, (_, b, c) in enumerate(stages)]
    for c in come:
        c.start()
    for a, b in zip(come, leave):
        a.wait()
        b.start()
    for c in leave:
        c.wait()


def per_device(diag_block, panel, panel_mask, slot_rows, trail):
    f32, i32 = jnp.float32, jnp.int32
    vm = lambda *shape: pltpu.VMEM(shape, f32)
    dma = lambda *shape: pltpu.SemaphoreType.DMA(shape)
    one = pltpu.SemaphoreType.DMA
    vmem = pl.BlockSpec(memory_space=pltpu.VMEM)
    hbm = pl.BlockSpec(memory_space=pl.ANY)
    shapes = (
        jax.ShapeDtypeStruct(diag_block.shape, f32),
        jax.ShapeDtypeStruct(panel.shape, f32),
        jax.ShapeDtypeStruct(trail.shape, f32),
    )
    slots = jnp.transpose(slot_rows, (1, 2, 0))
    bf = lambda *shape: pltpu.VMEM(shape, jnp.bfloat16)
    results = pl.pallas_call(
        kernel,
        out_shape=shapes,
        in_specs=[hbm] * 5,
        out_specs=(vmem, vmem, hbm),
        scratch_shapes=[
            vm(4, NK, NX, NY, 8, 128), vm(512, 512), vm(512, 512), vm(128, 128), vm(128, 128),
            vm(128, 512), bf(512, 512), bf(512, 512),
            vm(NX, TILES, RA, WIDTH), vm(TILES, NZ, SLAB, WIDTH),
            *[vm(TILES, RB, WIDTH) for _ in range(8)],
            vm(7, 8, RB, WIDTH), vm(15, NX, RA, WIDTH),
            vm(NX, NK, NY, RB, WIDTH), vm(NY, NK, NX, RA, WIDTH),
            bf(TILES, TW, WIDTH), bf(TILES, TW, WIDTH), bf(64, SLAB, WIDTH), bf(64, SLAB, WIDTH),
            vm(TILES, SLOTS, SLAB, TW), vm(TILES, SLOTS, SLAB, TW),
            vm(TILES, SLAB, WIDTH), pltpu.VMEM((2, TILES), i32), pltpu.VMEM(slots.shape, i32),
            pltpu.SMEM(slots.shape, i32), pltpu.VMEM((16, 64), i32), pltpu.SMEM((16, 64), i32),
            dma(4), dma(4), dma(4), dma(4, 3), dma(4), dma(4), one, one,
            dma(4, 2), dma(4, 2), dma(4, 2), dma(4, 2), one, dma(8), one, dma(8),
            dma(9), dma(4), dma(4),
        ],
        compiler_params=pltpu.CompilerParams(
            collective_id=0, has_side_effects=True, vmem_limit_bytes=58 * 1024 * 1024
        ),
        name="panels",
    )(diag_block, panel, panel_mask.T, slots, trail)
    return pl.pallas_call(
        deliver,
        out_shape=shapes,
        in_specs=[hbm] * 3,
        out_specs=(hbm,) * 3,
        scratch_shapes=[vm(*diag_block.shape), vm(*panel.shape), vm(*trail.shape), dma(6), dma(6)],
        compiler_params=pltpu.CompilerParams(vmem_limit_bytes=58 * 1024 * 1024),
        name="deliver",
    )(*results)


def solution(mesh):
    in_specs = (
        P("row", None),
        P("row", "col", None),
        P("row", None),
        P(),
        P("row", None, "col", None),
    )
    out_specs = (P("row", None), P("row", "col", None), P("row", None, "col", None))
    return jax.shard_map(
        per_device, mesh=mesh, in_specs=in_specs, out_specs=out_specs, check_vma=False
    )
```
